32 devices in a mesh: src: 4 (over x, core), gx: 4 (over z), yz: 2 (over y).
Axes of the slice: x: 2, y: 2, z: 4, core: 2. Of those that a mesh axis runs over, the one named last changes fastest.
Arguments:
- warm_start: float32 [2, 16, 128, 32, 256], P(None, 'src', 'gx', 'yz'), may hold values from -1 to 1, as said below
- conductivity: float32 [128, 32, 256], P('gx', 'yz'), may hold values from 0.2 to 5
- currents: float32 [16], P('src'), may hold values from 4 to 16
- electrodes: int32 [16, 2], P('src'), may hold values from 0 to 1048575
- receivers: int32 [256], replicated, may hold values from 0 to 1048575
- weights: float32 [16, 256], P('src'), may hold values from -24 to 24
Outputs:
- solutions: float32 [2, 16, 128, 32, 256], P(None, 'src', 'gx', 'yz')
- gradient: float32 [128, 32, 256], P('gx', 'yz', 'src')
The draws below stay inside these ranges and needn't reach their ends.
Inputs may be any that keep to these rules, and one draw needn't show every extreme that they name: `electrodes`: each entry is a linear cell index as in the reference program; two entries may name the same cell. `receivers`: each entry is a linear cell index as in the reference program; two entries may name the same cell. `warm_start`: previous potentials, finite.
All inputs are finite; a program needn't handle non-finite values.
Results may differ from the reference program's by a relative error of at most 0.0003.
Values sent between devices are 32-bit elements; how exact they have to be, the bound alone decides.
A program may use at most 128 MiB of HBM per device.

```python
import math
import jax
import jax.numpy as jnp
from jax import lax

NSRC = 16
NREC = 256
ITERS = 2
SRC_GRP = 4
NX = 128
NY = 32
NZ = 256


def sine_profile(count, wave):
    position = (jnp.arange(count, dtype=jnp.float32) + 0.5) / count
    return jnp.sin(math.pi * wave * position)


def draw_warm_start(key, part):
    shape = (2, NSRC, NX, NY, NZ)
    amp_key = jax.random.fold_in(key, 11)
    noise_key = jax.random.fold_in(key, 23)
    waves = ((1, 1, 1), (2, 1, 2), (1, 2, 1))
    amplitudes = 0.05 * jnp.clip(jax.random.normal(amp_key, (3, 2, NSRC), jnp.float32), -3.0, 3.0)
    field = jnp.zeros(shape, jnp.float32)
    for number, wave in enumerate(waves):
        mode = sine_profile(NX, wave[0])[:, None, None] * sine_profile(NY, wave[1])[None, :, None] * sine_profile(NZ, wave[2])[None, None, :]
        field = field + amplitudes[number][:, :, None, None, None] * mode[None, None]
    noise = 0.0001 * jnp.clip(jax.random.normal(noise_key, shape, jnp.float32), -6.0, 6.0)
    return (field + noise).astype(jnp.float32)


def place_ends(entries, key, least, top_value):
    longest = entries.shape.index(max(entries.shape))
    spots = []
    for shift in (0, 1):
        where = [jax.random.randint(jax.random.fold_in(key, axis), (), 0, length) for axis, length in enumerate(entries.shape)]
        where[longest] = (where[longest] + shift) % entries.shape[longest]
        spots.append(tuple(where))
    return entries.at[spots[0]].set(least).at[spots[1]].set(top_value)


def block_scale(rng, extent, split, smallest, high):
    def one(dim, parts):
        heights = jax.random.uniform(jax.random.fold_in(jax.random.fold_in(rng, 6), dim), (parts,), jnp.float32, smallest / len(split), high / len(split))
        return jnp.repeat(jnp.exp(heights), extent[dim] // parts).reshape((-1,) + (1,) * (len(extent) - dim - 1))

    loudness = one(*split[0])
    for cut in split[1:]:
        loudness = loudness * one(*cut)
    return loudness


def gaussian(rng, dims, width, limit, pieces=(), kind=jnp.bfloat16):
    level = block_scale(rng, dims, pieces, -0.22, 0.18) if pieces else 1.0
    array = jax.random.normal(rng, dims, jnp.float32) * width * level
    return jnp.minimum(jnp.maximum(array, -limit), limit).astype(kind)


def setup_inputs(seed: int = 0) -> dict:
    key_of = jax.random.split(jax.random.key(seed), 7)
    warm_start = draw_warm_start(jax.random.fold_in(key_of[6], 71), 0)
    conductivity = jnp.clip(jnp.exp(math.log(5.0) - 3.218876 * jax.random.uniform(key_of[1], (NX, NY, NZ), jnp.float32) ** block_scale(key_of[1], (NX, NY, NZ), ((0, 4), (1, 2)), -0.2, 0.2)), 0.2, 5.0)
    currents = jnp.clip(jnp.exp(math.log(16.0) - 1.3862944 * jax.random.uniform(key_of[2], (NSRC,), jnp.float32) ** block_scale(key_of[2], (NSRC,), ((0, 4),), -0.2, 0.2)), 4.0, 16.0)
    electrodes = place_ends(jax.random.randint(key_of[3], (NSRC, 2), 0, NX * NY * NZ), jax.random.fold_in(key_of[3], 1), 0, (NX * NY * NZ) - 1).astype(jnp.int32)
    receivers = place_ends(jax.random.randint(key_of[4], (NREC,), 0, NX * NY * NZ), jax.random.fold_in(key_of[4], 1), 0, (NX * NY * NZ) - 1).astype(jnp.int32)
    weights = gaussian(key_of[5], (NSRC, NREC), 4.0, 24.0, ((0, 4),), jnp.float32)
    return dict(warm_start=warm_start, conductivity=conductivity, currents=currents, electrodes=electrodes, receivers=receivers, weights=weights)


highest = lax.Precision.HIGHEST

def neighbours(padded):
    middle = padded[..., 1:-1, 1:-1, :]
    zeros = jnp.zeros(middle.shape[:-1] + (1,), middle.dtype)
    return (padded[..., 2:, 1:-1, :], padded[..., :-2, 1:-1, :], padded[..., 1:-1, 2:, :], padded[..., 1:-1, :-2, :], jnp.concatenate([middle[..., 1:], zeros], axis=-1), jnp.concatenate([zeros, middle[..., :-1]], axis=-1))

def pad_plane(field):
    widths = [(0, 0)] * (field.ndim - 3) + [(1, 1), (1, 1), (0, 0)]
    return jnp.pad(field, widths)

def apply(padded, faces, diagonal):
    field = padded[..., 1:-1, 1:-1, :]
    total = diagonal * field
    for weight, near in zip(faces, neighbours(padded)):
        total = total - weight * near
    return total

def gram(left, right):
    return jnp.einsum('axyz,bxyz->ab', left, right, precision=highest)

def combine(coef, field):
    return jnp.einsum('ab,axyz->bxyz', coef, field, precision=highest)

def solve_small(matrix, rhs):
    factor = jnp.linalg.cholesky(matrix)
    middle = lax.linalg.triangular_solve(factor, rhs, left_side=True, lower=True)
    return lax.linalg.triangular_solve(factor, middle, left_side=True, lower=True, transpose_a=True)

def local_gradient(padded_solution, count):
    field = padded_solution[:, 1:-1, 1:-1, :]
    forward = field[:count]
    adjoint = field[count:]
    total = jnp.zeros(field.shape[1:], jnp.float32)
    for near_fwd, near_adj in zip(neighbours(padded_solution[:count]), neighbours(padded_solution[count:])):
        total = total + jnp.sum((forward - near_fwd) * (adjoint - near_adj), axis=0)
    return -0.5 * total

def reference(warm_start, conductivity, currents, electrodes, receivers, weights):
    faces = tuple((0.5 * (conductivity + near) for near in neighbours(pad_plane(conductivity))))
    diagonal = faces[0]
    for weight in faces[1:]:
        diagonal = diagonal + weight

    def solve_group(group):
        start = (group * SRC_GRP).astype(jnp.int32)
        rows = start + jnp.arange(SRC_GRP, dtype=jnp.int32)
        local = jnp.arange(SRC_GRP, dtype=jnp.int32)
        field = jnp.zeros((2, SRC_GRP, NX * NY * NZ), jnp.float32)
        field = field.at[0, local, electrodes[rows, 0]].add(currents[rows])
        field = field.at[0, local, electrodes[rows, 1]].add(-currents[rows])
        field = field.at[1, local[:, None], receivers[None, :]].add(weights[rows])
        rhs = field.reshape(2 * SRC_GRP, NX, NY, NZ)
        solution = lax.dynamic_slice_in_dim(warm_start, start, SRC_GRP, 1).reshape(2 * SRC_GRP, NX, NY, NZ)
        residual = rhs - apply(pad_plane(solution), faces, diagonal)
        precond = residual / diagonal
        direction = precond
        inner = gram(residual, precond)
        for step in range(ITERS):
            image = apply(pad_plane(direction), faces, diagonal)
            curve = gram(direction, image)
            alpha = solve_small(curve, inner)
            solution = solution + combine(alpha, direction)
            residual = residual - combine(alpha, image)
            if step + 1 < ITERS:
                precond = residual / diagonal
                fresh = gram(residual, precond)
                beta = solve_small(inner, fresh)
                direction = precond + combine(beta, direction)
                inner = fresh
        return solution
    solved = lax.map(solve_group, jnp.arange(NSRC // SRC_GRP, dtype=jnp.int32))

    def accumulate(total, solution):
        return (total + local_gradient(pad_plane(solution), SRC_GRP), None)
    gradient, unused = lax.scan(accumulate, jnp.zeros((NX, NY, NZ), jnp.float32), solved)
    grouped = solved.reshape(NSRC // SRC_GRP, 2, SRC_GRP, NX, NY, NZ)
    solutions = jnp.moveaxis(grouped, 0, 1).reshape(2, NSRC, NX, NY, NZ)
    return (solutions, gradient)
```

```python
import functools
import jax
import jax.numpy as jnp
from jax import lax
from jax.experimental import pallas as pl
from jax.experimental.pallas import tpu as pltpu
from jax.sharding import PartitionSpec as P

MESH = pl.DeviceIdType.MESH
F32 = jnp.float32
COLS = 8
PAIRS = [(a, b) for a in range(COLS) for b in range(a, COLS)]


def matmul8(left, right):
    total = left[:, 0:1] * right[0:1, :]
    for k in range(1, COLS):
        total = total + left[:, k : k + 1] * right[k : k + 1, :]
    return total


def inverse8(matrix, row, lane):
    work = jnp.where(lane < COLS, matrix, jnp.where(lane - COLS == row, 1.0, 0.0))
    for k in range(COLS):
        scaled = work[k : k + 1, :] / work[k : k + 1, k : k + 1]
        work = jnp.where(row == k, scaled, work - work[:, k : k + 1] * scaled)
    return pltpu.roll(work, 128 - COLS, 1)


def kernel(
    sizes,
    warm, cond, currents, electrodes, receivers, weights,
    out_x, out_g,
    xv, pv, wv, yh, ysend, cv, ch, csend, cf, dv, iv, ybuf, onehot, table, gbuf, gp, grecv,
    load_sem, out_sem, send_sem, recv_sem, csend_sem, crecv_sem, gram_send, gram_recv, grad_send, grad_recv,
):
    nsrc, ngx, nyz, nx, ny, nz = sizes
    count = COLS // 2
    src, gx, yz = lax.axis_index("src"), lax.axis_index("gx"), lax.axis_index("yz")
    group = ngx * nyz
    me = gx * nyz + yz

    load_c = pltpu.make_async_copy(cond, cv.at[pl.ds(1, nx)], load_sem.at[0])
    load_x = pltpu.make_async_copy(warm, xv.at[:, pl.ds(1, nx)], load_sem.at[1])
    load_c.start()
    load_x.start()

    barrier = pltpu.get_barrier_semaphore()
    for o in range(1, group):
        to = lax.rem(me + o, group)
        pl.semaphore_signal(
            barrier, inc=1, device_id={"gx": to // nyz, "yz": lax.rem(to, nyz)}, device_id_type=MESH
        )
    for o in range(1, nsrc):
        pl.semaphore_signal(
            barrier, inc=1, device_id={"src": lax.rem(src + o, nsrc)}, device_id_type=MESH
        )

    edges = (gx > 0, gx < ngx - 1, yz > 0, yz < nyz - 1)
    fields = (xv, pv, wv)

    for side, plane in ((0, 0), (1, nx + 1)):
        @pl.when(jnp.logical_not(edges[side]))
        def _(plane=plane):
            cv[plane] = jnp.zeros((ny, nz), F32)
            for ref in fields:
                for c in range(COLS):
                    ref[c, plane] = jnp.zeros((ny, nz), F32)

    for side in (0, 1):
        @pl.when(jnp.logical_not(edges[2 + side]))
        def _(side=side):
            ch[side] = jnp.zeros((nx, nz), F32)
            for phase in range(3):
                for c in range(COLS):
                    yh[phase, side, c] = jnp.zeros((nx, nz), F32)

    def remote(source, target, send, recv, where):
        return pltpu.make_async_remote_copy(
            src_ref=source, dst_ref=target, send_sem=send, recv_sem=recv,
            device_id=where, device_id_type=MESH,
        )

    def x_copies(source, phase):
        def cut(plane):
            return source.at[plane] if phase == 3 else source.at[:, plane]
        if phase == 3:
            send, recv = csend_sem, crecv_sem
        else:
            send, recv = send_sem.at[phase], recv_sem.at[phase]
        return (
            (remote(cut(nx), cut(0), send.at[0], recv.at[0], {"gx": jnp.minimum(gx + 1, ngx - 1)}), edges[1], edges[0]),
            (remote(cut(1), cut(nx + 1), send.at[1], recv.at[1], {"gx": jnp.maximum(gx - 1, 0)}), edges[0], edges[1]),
        )

    def y_copies(phase):
        if phase == 3:
            send, recv, out, into = csend_sem, crecv_sem, csend, ch
        else:
            send, recv, out, into = send_sem.at[phase], recv_sem.at[phase], ysend.at[phase], yh.at[phase]
        return (
            (remote(out.at[1], into.at[0], send.at[2], recv.at[2], {"yz": jnp.minimum(yz + 1, nyz - 1)}), edges[3], edges[2]),
            (remote(out.at[0], into.at[1], send.at[3], recv.at[3], {"yz": jnp.maximum(yz - 1, 0)}), edges[2], edges[3]),
        )

    def start(copies):
        for copy, sends, _ in copies:
            pl.when(sends)(copy.start)

    def arrive(copies):
        for copy, _, receives in copies:
            pl.when(receives)(copy.wait_recv)

    def finish(copies):
        for copy, sends, _ in copies:
            pl.when(sends)(copy.wait_send)

    pl.semaphore_wait(barrier, group - 1 + nsrc - 1)

    load_c.wait()
    c_x = x_copies(cv, 3)
    start(c_x)
    for x in range(nx):
        csend[0, x : x + 1] = cv[x + 1, 0:1]
        csend[1, x : x + 1] = cv[x + 1, ny - 1 : ny]
    c_y = y_copies(3)
    start(c_y)

    load_x.wait()
    x_x = x_copies(xv, 0)

    @pl.loop(0, nx)
    def _(x):
        for c in range(COLS):
            ysend[0, 0, c, pl.ds(x, 1)] = xv[c, x + 1, 0:1]
            ysend[0, 1, c, pl.ds(x, 1)] = xv[c, x + 1, ny - 1 : ny]

    x_y = y_copies(0)
    start(x_y)
    start(x_x)

    row = lax.broadcasted_iota(jnp.int32, (ny, nz), 0)
    lane = lax.broadcasted_iota(jnp.int32, (ny, nz), 1)

    span = nyz * ny * nz
    place = receivers[...]
    where_x = place // span - gx * nx
    where_y = lax.rem(place, span) // nz - yz * ny
    inside = (where_x >= 0) & (where_x < nx) & (where_y >= 0) & (where_y < ny)
    line = jnp.where(inside, where_x * ny + where_y, -1)
    nrec = place.shape[1]
    spot = jnp.broadcast_to(lax.rem(place, nz), (nz, nrec))
    onehot[...] = jnp.where(
        lax.broadcasted_iota(jnp.int32, (nz, nrec), 0) == spot, 1.0, 0.0
    ).astype(jnp.bfloat16)
    step = 4
    rows = lax.broadcasted_iota(jnp.int32, (step * ny, nrec), 0)

    @pl.loop(0, nx // step)
    def _(i):
        match = rows + i * (step * ny) == line
        for s in range(count):
            value = weights[s : s + 1]
            total = None
            for part in range(3):
                piece = value.astype(jnp.bfloat16).astype(F32)
                value = value - piece
                term = lax.dot_general(
                    jnp.where(match, piece, 0.0).astype(jnp.bfloat16), onehot[...],
                    (((1,), (1,)), ((), ())), preferred_element_type=F32,
                )
                total = term if total is None else total + term
            for j in range(step):
                pv[count + s, i * step + j + 1] = total[j * ny : (j + 1) * ny]

    arrive(c_x)
    arrive(c_y)

    @pl.loop(0, nx)
    def _(x):
        mid = cv[x + 1]
        near = (
            cv[x + 2],
            cv[x],
            jnp.where(row == ny - 1, ch[1, pl.ds(x, 1)], pltpu.roll(mid, ny - 1, 0)),
            jnp.where(row == 0, ch[0, pl.ds(x, 1)], pltpu.roll(mid, 1, 0)),
            jnp.where(lane == nz - 1, 0.0, pltpu.roll(mid, nz - 1, 1)),
            jnp.where(lane == 0, 0.0, pltpu.roll(mid, 1, 1)),
        )
        faces = [0.5 * (mid + value) for value in near]
        diagonal = faces[0]
        for value in faces[1:]:
            diagonal = diagonal + value
        inverse = 1.0 / diagonal
        dv[x] = diagonal
        iv[x] = inverse
        faces[4] = jnp.where(lane == nz - 1, 0.0, faces[4])
        faces[5] = jnp.where(lane == 0, 0.0, faces[5])
        for j in range(6):
            cf[j, x] = faces[j] * inverse

    def around(phase, c, x):
        ref = fields[phase]
        field = ref[c, x + 1]
        above = jnp.where(row == ny - 1, yh[phase, 1, c, pl.ds(x, 1)], pltpu.roll(field, ny - 1, 0))
        below = jnp.where(row == 0, yh[phase, 0, c, pl.ds(x, 1)], pltpu.roll(field, 1, 0))
        total = cf[0, x] * ref[c, x + 2] + cf[1, x] * ref[c, x]
        total = total + cf[2, x] * above
        total = total + cf[3, x] * below
        total = total + cf[4, x] * pltpu.roll(field, nz - 1, 1)
        total = total + cf[5, x] * pltpu.roll(field, 1, 1)
        return field, total

    arrive(x_x)
    arrive(x_y)

    @pl.loop(0, nx)
    def _(x):
        cell = row * nz + lane + ((gx * nx + x) * span + yz * (ny * nz))
        inverse = iv[x]
        for c in range(COLS):
            field, total = around(0, c, x)
            if c < count:
                amount = currents[c]
                source = jnp.where(cell == electrodes[c, 0], amount, 0.0) - jnp.where(
                    cell == electrodes[c, 1], amount, 0.0
                )
            else:
                source = pv[c, x + 1]
            value = source * inverse - field + total
            pv[c, x + 1] = value
            ysend[1, 0, c, pl.ds(x, 1)] = value[0:1]
            ysend[1, 1, c, pl.ds(x, 1)] = value[ny - 1 : ny]

    p_x, p_y = x_copies(pv, 1), y_copies(1)
    start(p_y)
    start(p_x)

    def products(acc, x, left, right):
        acc = list(acc)
        for yb in range(ny // 8):
            for zb in range(nz // 128):
                cut = (slice(yb * 8, yb * 8 + 8), slice(zb * 128, zb * 128 + 128))
                scale = dv[(x,) + cut]
                lefts = [left[(a, x + 1) + cut] * scale for a in range(COLS)]
                if right is ybuf:
                    rights = [right[(b,) + cut] for b in range(COLS)]
                else:
                    rights = [right[(b, x + 1) + cut] for b in range(COLS)]
                for i, (a, b) in enumerate(PAIRS):
                    acc[i] = acc[i] + lefts[a] * rights[b]
        return tuple(acc)

    zeros = tuple(jnp.zeros((8, 128), F32) for _ in PAIRS)
    row8 = lax.broadcasted_iota(jnp.int32, (8, 128), 0)
    lane8 = lax.broadcasted_iota(jnp.int32, (8, 128), 1)

    def collect(acc):
        sums = {}
        for (a, b), value in zip(PAIRS, acc):
            sums[a, b] = sums[b, a] = jnp.sum(value, axis=0, keepdims=True)
        matrix = jnp.zeros((8, 128), F32)
        for a in range(COLS):
            block = jnp.zeros((8, 128), F32)
            for b in range(COLS):
                block = jnp.where(row8 == b, sums[a, b], block)
            matrix = jnp.where(lane8 == a, jnp.sum(block, axis=1, keepdims=True), matrix)
        return matrix

    def gram(left, right):
        return collect(lax.fori_loop(0, nx, lambda x, acc: products(acc, x, left, right), zeros))

    mine = gram(pv, pv)

    arrive(p_x)
    arrive(p_y)

    @pl.loop(0, nx)
    def _(x):
        for c in range(COLS):
            field, total = around(1, c, x)
            value = field - total
            wv[c, x + 1] = value
            ysend[2, 0, c, pl.ds(x, 1)] = value[0:1]
            ysend[2, 1, c, pl.ds(x, 1)] = value[ny - 1 : ny]

    w_x, w_y = x_copies(wv, 2), y_copies(2)
    start(w_y)
    start(w_x)

    mine = mine + pltpu.roll(gram(pv, wv), 8, 1)
    mine = mine + pltpu.roll(gram(wv, wv), 16, 1)

    arrive(w_x)
    arrive(w_y)

    def last(x, acc):
        for c in range(COLS):
            field, total = around(2, c, x)
            ybuf[c] = field - total
        return products(acc, x, wv, ybuf)

    mine = mine + pltpu.roll(collect(lax.fori_loop(0, nx, last, zeros)), 24, 1)

    gbuf[me] = mine
    sums = []
    for o in range(1, group):
        to = lax.rem(me + o, group)
        copy = remote(
            gbuf.at[me], gbuf.at[me], gram_send.at[o - 1], gram_recv.at[o - 1],
            {"gx": to // nyz, "yz": lax.rem(to, nyz)},
        )
        copy.start()
        sums.append(copy)
    for copy in sums:
        copy.wait_recv()
    total = gbuf[0]
    for o in range(1, group):
        total = total + gbuf[o]

    first = total
    curve = pltpu.roll(total, 120, 1)
    second = pltpu.roll(total, 112, 1)
    third = pltpu.roll(total, 104, 1)
    unit = jnp.where(row8 == lane8, 1.0, 0.0)
    curve_inv = inverse8(curve, row8, lane8)
    first_inv = inverse8(first, row8, lane8)
    alpha = matmul8(curve_inv, first)
    alpha_t = matmul8(first, curve_inv)
    second_alpha = matmul8(second, alpha)
    fresh = first - matmul8(curve, alpha) - matmul8(alpha_t, curve) + matmul8(alpha_t, second_alpha)
    mixed = unit + matmul8(first_inv, fresh)
    mixed_t = unit + matmul8(fresh, first_inv)
    upper = matmul8(curve, mixed) - second_alpha
    lower = matmul8(second, mixed) - matmul8(third, alpha)
    curve_next = matmul8(mixed_t, upper) - matmul8(alpha_t, lower)
    alpha_next = matmul8(inverse8(curve_next, row8, lane8), fresh)
    coef_p = alpha + matmul8(mixed, alpha_next)
    coef_w = -matmul8(alpha, alpha_next)
    for a in range(COLS):
        for b in range(COLS):
            table[a * COLS + b] = jnp.broadcast_to(coef_p[a : a + 1, b : b + 1], (8, 128))
            table[(COLS + a) * COLS + b] = jnp.broadcast_to(coef_w[a : a + 1, b : b + 1], (8, 128))

    def combine(xref, pref, wref, index, cuts):
        starts = [[ref[(a,) + index + cut] for a in range(COLS) for cut in cuts] for ref in (pref, wref)]
        n = len(cuts)
        for b in range(COLS):
            acc = [xref[(b,) + index + cut] for cut in cuts]
            for part in range(2):
                for a in range(COLS):
                    factor = table[(part * COLS + a) * COLS + b]
                    acc = [acc[j] + starts[part][a * n + j] * factor for j in range(n)]
            for j, cut in enumerate(cuts):
                xref[(b,) + index + cut] = acc[j]

    finish(x_x)
    lanes = [slice(zb * 128, zb * 128 + 128) for zb in range(nz // 128)]

    @pl.loop(0, nx + 2)
    def _(x):
        for yb in range(ny // 8):
            combine(xv, pv, wv, (x,), [(slice(yb * 8, yb * 8 + 8), cut) for cut in lanes])

    for side in (0, 1):
        @pl.when(edges[2 + side])
        def _(side=side):
            @pl.loop(0, nx // 8)
            def _(i):
                combine(
                    yh.at[0, side], yh.at[1, side], yh.at[2, side], (),
                    [(pl.ds(pl.multiple_of(i * 8, 8), 8), cut) for cut in lanes],
                )

    store_x = pltpu.make_async_copy(xv.at[:, pl.ds(1, nx)], out_x, out_sem)

    store_x.start()

    half = lane8 < 64
    chunks = 2
    length = nx // chunks
    sent = []

    def face(x):
        total = None
        for s in range(count):
            term = (xv[s, x] - xv[s, x + 1]) * (xv[count + s, x] - xv[count + s, x + 1])
            total = term if total is None else total + term
        return total

    def planes(x, before):
        after = face(x + 1)
        fy = fz = edge_y = edge_z = None
        for s in range(count):
            u, w = xv[s, x + 1], xv[count + s, x + 1]
            uy = u - jnp.where(row == ny - 1, yh[0, 1, s, pl.ds(x, 1)], pltpu.roll(u, ny - 1, 0))
            wy = w - jnp.where(row == ny - 1, yh[0, 1, count + s, pl.ds(x, 1)], pltpu.roll(w, ny - 1, 0))
            uz = u - jnp.where(lane == nz - 1, 0.0, pltpu.roll(u, nz - 1, 1))
            wz = w - jnp.where(lane == nz - 1, 0.0, pltpu.roll(w, nz - 1, 1))
            low = (u[0:1] - yh[0, 0, s, pl.ds(x, 1)]) * (w[0:1] - yh[0, 0, count + s, pl.ds(x, 1)])
            terms = (uy * wy, uz * wz, low, u * w)
            if fy is None:
                fy, fz, edge_y, edge_z = terms
            else:
                fy, fz, edge_y, edge_z = (p + q for p, q in zip((fy, fz, edge_y, edge_z), terms))
        total = before + after
        total = total + fy + jnp.where(row == 0, edge_y, pltpu.roll(fy, 1, 0))
        total = total + fz + jnp.where(lane == 0, edge_z, pltpu.roll(fz, 1, 1))
        total = -0.5 * total
        for t in range(nz // 128):
            top, low = total[0:8, lanes[t]], total[8:16, lanes[t]]
            gp[2 * t, x] = jnp.where(half, top, pltpu.roll(low, 64, 1))
            gp[2 * t + 1, x] = jnp.where(half, pltpu.roll(top, 64, 1), low)
        return after

    before = face(0)
    for k in range(chunks):
        before = lax.fori_loop(k * length, (k + 1) * length, planes, before)
        for o in range(1, nsrc):
            to = lax.rem(src + o, nsrc)
            part = pl.ds(k * length, length)
            copy = remote(
                gp.at[to, part], grecv.at[o - 1, part],
                grad_send.at[k, o - 1], grad_recv.at[k, o - 1], {"src": to},
            )
            copy.start()
            sent.append(copy)

    for k in range(chunks):
        for o in range(1, nsrc):
            sent[k * (nsrc - 1) + o - 1].wait_recv()

        @pl.loop(k * length, (k + 1) * length)
        def _(x):
            total = gp[src, x]
            for o in range(nsrc - 1):
                total = total + grecv[o, x]
            out_g[x, 0:8] = total[:, 0:64]
            out_g[x, 8:16] = pltpu.roll(total, 64, 1)[:, 0:64]

    for copies in (c_x, c_y, x_y, p_x, p_y, w_x, w_y):
        finish(copies)
    for copy in sums + sent:
        copy.wait_send()
    store_x.wait()


def on_device(sizes, warm_start, conductivity, currents, electrodes, receivers, weights):
    nsrc, ngx, nyz, nx, ny, nz = sizes
    group = ngx * nyz
    nrec = receivers.shape[0]
    dma = pltpu.SemaphoreType.DMA
    vmem = pl.BlockSpec(memory_space=pltpu.VMEM)
    smem = pl.BlockSpec(memory_space=pltpu.SMEM)
    hbm = pl.BlockSpec(memory_space=pl.ANY)
    block = pltpu.VMEM((COLS, nx + 2, ny, nz), F32)
    cells = COLS * nx * ny * nz
    solutions, gradient = pl.pallas_call(
        functools.partial(kernel, sizes),
        out_shape=(
            jax.ShapeDtypeStruct((COLS, nx, ny, nz), F32),
            jax.ShapeDtypeStruct((nx, ny, nz // nsrc), F32),
        ),
        in_specs=[hbm, hbm, smem, smem, vmem, vmem],
        out_specs=(hbm, vmem),
        scratch_shapes=[
            block, block, block,
            pltpu.VMEM((3, 2, COLS, nx, nz), F32),
            pltpu.VMEM((3, 2, COLS, nx, nz), F32),
            pltpu.VMEM((nx + 2, ny, nz), F32),
            pltpu.VMEM((2, nx, nz), F32),
            pltpu.VMEM((2, nx, nz), F32),
            pltpu.VMEM((6, nx, ny, nz), F32),
            pltpu.VMEM((nx, ny, nz), F32),
            pltpu.VMEM((nx, ny, nz), F32),
            pltpu.VMEM((COLS, ny, nz), F32),
            pltpu.VMEM((nz, nrec), jnp.bfloat16),
            pltpu.VMEM((2 * COLS * COLS, 8, 128), F32),
            pltpu.VMEM((group, 8, 128), F32),
            pltpu.VMEM((nsrc, nx, 8, 128), F32),
            pltpu.VMEM((nsrc - 1, nx, 8, 128), F32),
            dma((2,)), dma,
            dma((3, 4)), dma((3, 4)),
            dma((4,)), dma((4,)),
            dma((group - 1,)), dma((group - 1,)),
            dma((2, nsrc - 1)), dma((2, nsrc - 1)),
        ],
        compiler_params=pltpu.CompilerParams(
            collective_id=0, has_side_effects=True, vmem_limit_bytes=48 * 1024 * 1024
        ),
        cost_estimate=pl.CostEstimate(flops=300 * cells, bytes_accessed=8 * cells, transcendentals=0),
    )(
        warm_start.reshape((COLS, nx, ny, nz)), conductivity, currents, electrodes,
        receivers.reshape(1, nrec), weights,
    )
    return solutions.reshape(warm_start.shape), gradient


def solution(mesh):
    nsrc, ngx, nyz = (mesh.shape[name] for name in ("src", "gx", "yz"))

    def run(warm_start, conductivity, *rest):
        gx, gy, gz = conductivity.shape
        sizes = (nsrc, ngx, nyz, gx // ngx, gy // nyz, gz)
        return jax.shard_map(
            functools.partial(on_device, sizes),
            mesh=mesh,
            in_specs=(
                P(None, "src", "gx", "yz", None),
                P("gx", "yz", None),
                P("src"),
                P("src", None),
                P(),
                P("src", None),
            ),
            out_specs=(P(None, "src", "gx", "yz", None), P("gx", "yz", "src")),
            check_vma=False,
        )(warm_start, conductivity, *rest)

    return run
```

```python
import functools
import jax
import jax.numpy as jnp
from jax import lax
from jax.experimental import pallas as pl
from jax.experimental.pallas import tpu as pltpu
from jax.sharding import PartitionSpec as P

MESH = pl.DeviceIdType.MESH
F32 = jnp.float32
COLS = 8
PAIRS = [(a, b) for a in range(COLS) for b in range(a, COLS)]


def matmul8(left, right):
    total = left[:, 0:1] * right[0:1, :]
    for k in range(1, COLS):
        total = total + left[:, k : k + 1] * right[k : k + 1, :]
    return total


def inverse8(matrix, row, lane):
    work = jnp.where(lane < COLS, matrix, jnp.where(lane - COLS == row, 1.0, 0.0))
    for k in range(COLS):
        scaled = work[k : k + 1, :] / work[k : k + 1, k : k + 1]
        work = jnp.where(row == k, scaled, work - work[:, k : k + 1] * scaled)
    return pltpu.roll(work, 128 - COLS, 1)


def kernel(
    sizes,
    warm, cond, currents_in, electrodes_in, receivers_in, weights_in,
    out_x, out_g,
    currents, electrodes, receivers, weights,
    xv, pv, wv, yh, ysend, cv, ch, csend, cf, dv, iv, ybuf, onehot, table, gbuf, gp, grecv,
    load_sem, out_sem, send_sem, recv_sem, ysend_sem, yrecv_sem, csend_sem, crecv_sem, gram_send, gram_recv, grad_send, grad_recv,
):
    nsrc, ngx, nyz, nx, ny, nz = sizes
    count = COLS // 2
    src, gx, yz = lax.axis_index("src"), lax.axis_index("gx"), lax.axis_index("yz")
    group = ngx * nyz
    me = gx * nyz + yz

    load_c = pltpu.make_async_copy(cond, cv.at[pl.ds(1, nx)], load_sem.at[0])
    load_x = pltpu.make_async_copy(warm, xv.at[:, pl.ds(1, nx)], load_sem.at[1])
    small = [
        pltpu.make_async_copy(source, target, load_sem.at[2 + i])
        for i, (source, target) in enumerate((
            (currents_in, currents), (electrodes_in, electrodes), (receivers_in, receivers), (weights_in, weights),
        ))
    ]
    load_c.start()
    for copy in small:
        copy.start()
    load_x.start()

    barrier = pltpu.get_barrier_semaphore()
    for o in range(1, group):
        to = lax.rem(me + o, group)
        pl.semaphore_signal(
            barrier, inc=1, device_id={"gx": to // nyz, "yz": lax.rem(to, nyz)}, device_id_type=MESH
        )
    for o in range(1, nsrc):
        pl.semaphore_signal(
            barrier, inc=1, device_id={"src": lax.rem(src + o, nsrc)}, device_id_type=MESH
        )

    edges = (gx > 0, gx < ngx - 1, yz > 0, yz < nyz - 1)
    fields = (xv, pv, wv)
    parts = 4
    width = nx // parts

    for side, plane in ((0, 0), (1, nx + 1)):
        @pl.when(jnp.logical_not(edges[side]))
        def _(plane=plane):
            cv[plane] = jnp.zeros((ny, nz), F32)
            for ref in fields:
                for c in range(COLS):
                    ref[c, plane] = jnp.zeros((ny, nz), F32)

    for side in (0, 1):
        @pl.when(jnp.logical_not(edges[2 + side]))
        def _(side=side):
            ch[side] = jnp.zeros((nx, nz), F32)
            for phase in range(3):
                for c in range(COLS):
                    yh[phase, side, c] = jnp.zeros((nx, nz), F32)

    def remote(source, target, send, recv, where):
        return pltpu.make_async_remote_copy(
            src_ref=source, dst_ref=target, send_sem=send, recv_sem=recv,
            device_id=where, device_id_type=MESH,
        )

    def x_copies(source, phase):
        def cut(plane):
            return source.at[plane] if phase == 3 else source.at[:, plane]

        def mine(plane):
            return warm.at[:, plane - 1] if phase == 0 else cut(plane)
        if phase == 3:
            send, recv = csend_sem, crecv_sem
        else:
            send, recv = send_sem.at[phase], recv_sem.at[phase]
        return (
            (remote(mine(nx), cut(0), send.at[0], recv.at[0], {"gx": jnp.minimum(gx + 1, ngx - 1)}), edges[1], edges[0]),
            (remote(mine(1), cut(nx + 1), send.at[1], recv.at[1], {"gx": jnp.maximum(gx - 1, 0)}), edges[0], edges[1]),
        )

    after_y, before_y = {"yz": jnp.minimum(yz + 1, nyz - 1)}, {"yz": jnp.maximum(yz - 1, 0)}

    def c_copies():
        return (
            (remote(csend.at[1], ch.at[0], csend_sem.at[2], crecv_sem.at[2], after_y), edges[3], edges[2]),
            (remote(csend.at[0], ch.at[1], csend_sem.at[3], crecv_sem.at[3], before_y), edges[2], edges[3]),
        )

    def y_copies(phase, q):
        part = pl.ds(pl.multiple_of(q * width, 8), width)
        out, into = ysend.at[phase], yh.at[phase]
        send, recv = ysend_sem.at[phase, q], yrecv_sem.at[phase, q]
        return (
            (remote(out.at[1, :, part], into.at[0, :, part], send.at[0], recv.at[0], after_y), edges[3], edges[2]),
            (remote(out.at[0, :, part], into.at[1, :, part], send.at[1], recv.at[1], before_y), edges[2], edges[3]),
        )

    def sweep(phase, plane, carry):
        def part(k, carry):
            q = lax.rem(parts - k, parts)
            arrive(y_copies(phase, q))
            source = fields[phase]

            @pl.when(k == 0)
            def _():
                arrive(x_copies(source, phase)[:1])

            @pl.when(k == 1)
            def _():
                arrive(x_copies(source, phase)[1:])

            carry = lax.fori_loop(0, width, lambda i, c: plane(q * width + i, c), carry)
            if phase < 2:
                start(y_copies(phase + 1, q))
                target = fields[phase + 1]

                @pl.when(k == 0)
                def _():
                    start(x_copies(target, phase + 1)[1:])

                @pl.when(k == 1)
                def _():
                    start(x_copies(target, phase + 1)[:1])
            return carry

        return lax.fori_loop(0, parts, part, carry)

    def start(copies):
        for copy, sends, _ in copies:
            pl.when(sends)(copy.start)

    def arrive(copies):
        for copy, _, receives in copies:
            pl.when(receives)(copy.wait_recv)

    def finish(copies):
        for copy, sends, _ in copies:
            pl.when(sends)(copy.wait_send)

    pl.semaphore_wait(barrier, group - 1 + nsrc - 1)

    x_x = x_copies(xv, 0)
    start(x_x)
    load_c.wait()
    c_x = x_copies(cv, 3)
    start(c_x)
    for x in range(nx):
        csend[0, x : x + 1] = cv[x + 1, 0:1]
        csend[1, x : x + 1] = cv[x + 1, ny - 1 : ny]
    c_y = c_copies()
    start(c_y)

    load_x.wait()

    @pl.loop(0, nx)
    def _(x):
        for c in range(COLS):
            ysend[0, 0, c, pl.ds(x, 1)] = xv[c, x + 1, 0:1]
            ysend[0, 1, c, pl.ds(x, 1)] = xv[c, x + 1, ny - 1 : ny]

    for q in (0, 3, 2, 1):
        start(y_copies(0, q))
    for copy in small:
        copy.wait()

    row = lax.broadcasted_iota(jnp.int32, (ny, nz), 0)
    lane = lax.broadcasted_iota(jnp.int32, (ny, nz), 1)

    span = nyz * ny * nz
    place = receivers[...]
    where_x = place // span - gx * nx
    where_y = lax.rem(place, span) // nz - yz * ny
    inside = (where_x >= 0) & (where_x < nx) & (where_y >= 0) & (where_y < ny)
    line = jnp.where(inside, where_x * ny + where_y, -1)
    nrec = place.shape[1]
    spot = jnp.broadcast_to(lax.rem(place, nz), (nz, nrec))
    onehot[...] = jnp.where(
        lax.broadcasted_iota(jnp.int32, (nz, nrec), 0) == spot, 1.0, 0.0
    ).astype(jnp.bfloat16)
    step = 4
    rows = lax.broadcasted_iota(jnp.int32, (step * ny, nrec), 0)

    @pl.loop(0, nx // step)
    def _(i):
        match = rows + i * (step * ny) == line
        values = [weights[s : s + 1] for s in range(count)]
        total = None
        for part in range(2):
            pieces = [value.astype(jnp.bfloat16).astype(F32) for value in values]
            values = [value - piece for value, piece in zip(values, pieces)]
            term = lax.dot_general(
                jnp.concatenate([jnp.where(match, piece, 0.0).astype(jnp.bfloat16) for piece in pieces], axis=0),
                onehot[...], (((1,), (1,)), ((), ())), preferred_element_type=F32,
            )
            total = term if total is None else total + term
        for s in range(count):
            for j in range(step):
                first = (s * step + j) * ny
                pv[count + s, i * step + j + 1] = total[first : first + ny]

    arrive(c_x)
    arrive(c_y)

    @pl.loop(0, nx)
    def _(x):
        mid = cv[x + 1]
        near = (
            cv[x + 2],
            cv[x],
            jnp.where(row == ny - 1, ch[1, pl.ds(x, 1)], pltpu.roll(mid, ny - 1, 0)),
            jnp.where(row == 0, ch[0, pl.ds(x, 1)], pltpu.roll(mid, 1, 0)),
            jnp.where(lane == nz - 1, 0.0, pltpu.roll(mid, nz - 1, 1)),
            jnp.where(lane == 0, 0.0, pltpu.roll(mid, 1, 1)),
        )
        faces = [0.5 * (mid + value) for value in near]
        diagonal = faces[0]
        for value in faces[1:]:
            diagonal = diagonal + value
        inverse = 1.0 / diagonal
        dv[x] = diagonal
        iv[x] = inverse
        faces[4] = jnp.where(lane == nz - 1, 0.0, faces[4])
        faces[5] = jnp.where(lane == 0, 0.0, faces[5])
        for j in range(6):
            cf[j, x] = faces[j] * inverse

    def around(phase, c, x):
        ref = fields[phase]
        field = ref[c, x + 1]
        above = jnp.where(row == ny - 1, yh[phase, 1, c, pl.ds(x, 1)], pltpu.roll(field, ny - 1, 0))
        below = jnp.where(row == 0, yh[phase, 0, c, pl.ds(x, 1)], pltpu.roll(field, 1, 0))
        total = cf[0, x] * ref[c, x + 2] + cf[1, x] * ref[c, x]
        total = total + cf[2, x] * above
        total = total + cf[3, x] * below
        total = total + cf[4, x] * pltpu.roll(field, nz - 1, 1)
        total = total + cf[5, x] * pltpu.roll(field, 1, 1)
        return field, total

    def plane_p(x, carry):
        cell = row * nz + lane + ((gx * nx + x) * span + yz * (ny * nz))
        inverse = iv[x]
        for c in range(COLS):
            field, total = around(0, c, x)
            if c < count:
                amount = currents[c]
                source = jnp.where(cell == electrodes[0, c], amount, 0.0) - jnp.where(
                    cell == electrodes[1, c], amount, 0.0
                )
            else:
                source = pv[c, x + 1]
            value = source * inverse - field + total
            pv[c, x + 1] = value
            ysend[1, 0, c, pl.ds(x, 1)] = value[0:1]
            ysend[1, 1, c, pl.ds(x, 1)] = value[ny - 1 : ny]

        return carry

    sweep(0, plane_p, 0)

    def products(acc, x, left, right):
        acc = list(acc)
        for yb in range(ny // 8):
            for zb in range(nz // 128):
                cut = (slice(yb * 8, yb * 8 + 8), slice(zb * 128, zb * 128 + 128))
                scale = dv[(x,) + cut]
                lefts = [left[(a, x + 1) + cut] * scale for a in range(COLS)]
                if right is ybuf:
                    rights = [right[(b,) + cut] for b in range(COLS)]
                else:
                    rights = [right[(b, x + 1) + cut] for b in range(COLS)]
                for i, (a, b) in enumerate(PAIRS):
                    acc[i] = acc[i] + lefts[a] * rights[b]
        return tuple(acc)

    zeros = tuple(jnp.zeros((8, 128), F32) for _ in PAIRS)
    row8 = lax.broadcasted_iota(jnp.int32, (8, 128), 0)
    lane8 = lax.broadcasted_iota(jnp.int32, (8, 128), 1)

    def collect(acc):
        sums = {}
        for (a, b), value in zip(PAIRS, acc):
            sums[a, b] = sums[b, a] = jnp.sum(value, axis=0, keepdims=True)
        matrix = jnp.zeros((8, 128), F32)
        for a in range(COLS):
            block = jnp.zeros((8, 128), F32)
            for b in range(COLS):
                block = jnp.where(row8 == b, sums[a, b], block)
            matrix = jnp.where(lane8 == a, jnp.sum(block, axis=1, keepdims=True), matrix)
        return matrix

    def gram(left, right):
        return collect(lax.fori_loop(0, nx, lambda x, acc: products(acc, x, left, right), zeros))

    mine = gram(pv, pv)

    def plane_w(x, carry):
        for c in range(COLS):
            field, total = around(1, c, x)
            value = field - total
            wv[c, x + 1] = value
            ysend[2, 0, c, pl.ds(x, 1)] = value[0:1]
            ysend[2, 1, c, pl.ds(x, 1)] = value[ny - 1 : ny]

        return carry

    sweep(1, plane_w, 0)

    mine = mine + pltpu.roll(gram(pv, wv), 8, 1)
    mine = mine + pltpu.roll(gram(wv, wv), 16, 1)

    def last(x, acc):
        for c in range(COLS):
            field, total = around(2, c, x)
            ybuf[c] = field - total
        return products(acc, x, wv, ybuf)

    mine = mine + pltpu.roll(collect(sweep(2, last, zeros)), 24, 1)

    gbuf[me] = mine
    sums = []
    for o in range(1, group):
        to = lax.rem(me + o, group)
        copy = remote(
            gbuf.at[me], gbuf.at[me], gram_send.at[o - 1], gram_recv.at[o - 1],
            {"gx": to // nyz, "yz": lax.rem(to, nyz)},
        )
        copy.start()
        sums.append(copy)
    for copy in sums:
        copy.wait_recv()
    total = gbuf[0]
    for o in range(1, group):
        total = total + gbuf[o]

    first = total
    curve = pltpu.roll(total, 120, 1)
    second = pltpu.roll(total, 112, 1)
    third = pltpu.roll(total, 104, 1)
    unit = jnp.where(row8 == lane8, 1.0, 0.0)
    curve_inv = inverse8(curve, row8, lane8)
    first_inv = inverse8(first, row8, lane8)
    alpha = matmul8(curve_inv, first)
    alpha_t = matmul8(first, curve_inv)
    second_alpha = matmul8(second, alpha)
    fresh = first - matmul8(curve, alpha) - matmul8(alpha_t, curve) + matmul8(alpha_t, second_alpha)
    mixed = unit + matmul8(first_inv, fresh)
    mixed_t = unit + matmul8(fresh, first_inv)
    upper = matmul8(curve, mixed) - second_alpha
    lower = matmul8(second, mixed) - matmul8(third, alpha)
    curve_next = matmul8(mixed_t, upper) - matmul8(alpha_t, lower)
    alpha_next = matmul8(inverse8(curve_next, row8, lane8), fresh)
    coef_p = alpha + matmul8(mixed, alpha_next)
    coef_w = -matmul8(alpha, alpha_next)
    for a in range(COLS):
        for b in range(COLS):
            table[a * COLS + b] = jnp.broadcast_to(coef_p[a : a + 1, b : b + 1], (8, 128))
            table[(COLS + a) * COLS + b] = jnp.broadcast_to(coef_w[a : a + 1, b : b + 1], (8, 128))

    def combine(xref, pref, wref, index, cuts):
        starts = [[ref[(a,) + index + cut] for a in range(COLS) for cut in cuts] for ref in (pref, wref)]
        n = len(cuts)
        for b in range(COLS):
            acc = [xref[(b,) + index + cut] for cut in cuts]
            for part in range(2):
                for a in range(COLS):
                    factor = table[(part * COLS + a) * COLS + b]
                    acc = [acc[j] + starts[part][a * n + j] * factor for j in range(n)]
            for j, cut in enumerate(cuts):
                xref[(b,) + index + cut] = acc[j]

    finish(x_x)
    lanes = [slice(zb * 128, zb * 128 + 128) for zb in range(nz // 128)]

    @pl.loop(0, nx + 2)
    def _(x):
        for yb in range(ny // 8):
            combine(xv, pv, wv, (x,), [(slice(yb * 8, yb * 8 + 8), cut) for cut in lanes])

    for side in (0, 1):
        @pl.when(edges[2 + side])
        def _(side=side):
            @pl.loop(0, nx // 8)
            def _(i):
                combine(
                    yh.at[0, side], yh.at[1, side], yh.at[2, side], (),
                    [(pl.ds(pl.multiple_of(i * 8, 8), 8), cut) for cut in lanes],
                )

    store_x = pltpu.make_async_copy(xv.at[:, pl.ds(1, nx)], out_x, out_sem)

    store_x.start()

    half = lane8 < 64
    chunks = 8
    length = nx // chunks

    def face(x):
        total = None
        for s in range(count):
            term = (xv[s, x] - xv[s, x + 1]) * (xv[count + s, x] - xv[count + s, x + 1])
            total = term if total is None else total + term
        return total

    def planes(x, before):
        after = face(x + 1)
        fy = fz = edge_y = edge_z = None
        for s in range(count):
            u, w = xv[s, x + 1], xv[count + s, x + 1]
            uy = u - jnp.where(row == ny - 1, yh[0, 1, s, pl.ds(x, 1)], pltpu.roll(u, ny - 1, 0))
            wy = w - jnp.where(row == ny - 1, yh[0, 1, count + s, pl.ds(x, 1)], pltpu.roll(w, ny - 1, 0))
            uz = u - jnp.where(lane == nz - 1, 0.0, pltpu.roll(u, nz - 1, 1))
            wz = w - jnp.where(lane == nz - 1, 0.0, pltpu.roll(w, nz - 1, 1))
            low = (u[0:1] - yh[0, 0, s, pl.ds(x, 1)]) * (w[0:1] - yh[0, 0, count + s, pl.ds(x, 1)])
            terms = (uy * wy, uz * wz, low, u * w)
            if fy is None:
                fy, fz, edge_y, edge_z = terms
            else:
                fy, fz, edge_y, edge_z = (p + q for p, q in zip((fy, fz, edge_y, edge_z), terms))
        total = before + after
        total = total + fy + jnp.where(row == 0, edge_y, pltpu.roll(fy, 1, 0))
        total = total + fz + jnp.where(lane == 0, edge_z, pltpu.roll(fz, 1, 1))
        total = -0.5 * total
        for t in range(nz // 128):
            top, low = total[0:8, lanes[t]], total[8:16, lanes[t]]
            gp[2 * t, x] = jnp.where(half, top, pltpu.roll(low, 64, 1))
            gp[2 * t + 1, x] = jnp.where(half, pltpu.roll(top, 64, 1), low)
        return after

    def grad_copies(k):
        part = pl.ds(k * length, length)
        for o in range(1, nsrc):
            to = lax.rem(src + o, nsrc)
            yield remote(
                gp.at[to, part], grecv.at[o - 1, part],
                grad_send.at[k, o - 1], grad_recv.at[k, o - 1], {"src": to},
            )

    def send_chunk(k, before):
        before = lax.fori_loop(k * length, (k + 1) * length, planes, before)
        for copy in grad_copies(k):
            copy.start()
        return before

    lax.fori_loop(0, chunks, send_chunk, face(0))

    @pl.loop(0, chunks)
    def _(k):
        for copy in grad_copies(k):
            copy.wait_recv()
        for i in range(length):
            x = k * length + i
            total = gp[src, x]
            for o in range(nsrc - 1):
                total = total + grecv[o, x]
            out_g[x, 0:8] = total[:, 0:64]
            out_g[x, 8:16] = pltpu.roll(total, 64, 1)[:, 0:64]

    @pl.loop(0, chunks)
    def _(k):
        for copy in grad_copies(k):
            copy.wait_send()

    for copies in (c_x, c_y, x_copies(pv, 1), x_copies(wv, 2)):
        finish(copies)
    for phase in range(3):
        for q in range(parts):
            finish(y_copies(phase, q))
    for copy in sums:
        copy.wait_send()
    store_x.wait()


def on_device(sizes, warm_start, conductivity, currents, electrodes, receivers, weights):
    nsrc, ngx, nyz, nx, ny, nz = sizes
    group = ngx * nyz
    nrec = receivers.shape[0]
    count = weights.shape[0]
    dma = pltpu.SemaphoreType.DMA
    vmem = pl.BlockSpec(memory_space=pltpu.VMEM)
    hbm = pl.BlockSpec(memory_space=pltpu.HBM)
    block = pltpu.VMEM((COLS, nx + 2, ny, nz), F32)
    cells = COLS * nx * ny * nz
    solutions, gradient = pl.pallas_call(
        functools.partial(kernel, sizes),
        out_shape=(
            jax.ShapeDtypeStruct((COLS, nx, ny, nz), F32),
            jax.ShapeDtypeStruct((nx, ny, nz // nsrc), F32),
        ),
        in_specs=[hbm] * 6,
        out_specs=(hbm, vmem),
        scratch_shapes=[
            pltpu.SMEM((count,), F32),
            pltpu.SMEM((2, count), jnp.int32),
            pltpu.VMEM((1, nrec), jnp.int32),
            pltpu.VMEM((count, nrec), F32),
            block, block, block,
            pltpu.VMEM((3, 2, COLS, nx, nz), F32),
            pltpu.VMEM((3, 2, COLS, nx, nz), F32),
            pltpu.VMEM((nx + 2, ny, nz), F32),
            pltpu.VMEM((2, nx, nz), F32),
            pltpu.VMEM((2, nx, nz), F32),
            pltpu.VMEM((6, nx, ny, nz), F32),
            pltpu.VMEM((nx, ny, nz), F32),
            pltpu.VMEM((nx, ny, nz), F32),
            pltpu.VMEM((COLS, ny, nz), F32),
            pltpu.VMEM((nz, nrec), jnp.bfloat16),
            pltpu.VMEM((2 * COLS * COLS, 8, 128), F32),
            pltpu.VMEM((group, 8, 128), F32),
            pltpu.VMEM((nsrc, nx, 8, 128), F32),
            pltpu.VMEM((nsrc - 1, nx, 8, 128), F32),
            dma((6,)), dma,
            dma((3, 2)), dma((3, 2)),
            dma((3, 4, 2)), dma((3, 4, 2)),
            dma((4,)), dma((4,)),
            dma((group - 1,)), dma((group - 1,)),
            dma((8, nsrc - 1)), dma((8, nsrc - 1)),
        ],
        compiler_params=pltpu.CompilerParams(
            collective_id=0, has_side_effects=True, vmem_limit_bytes=64 * 1024 * 1024
        ),
        cost_estimate=pl.CostEstimate(flops=300 * cells, bytes_accessed=8 * cells, transcendentals=0),
    )(
        warm_start.reshape((COLS, nx, ny, nz)), conductivity, currents, electrodes.T,
        receivers.reshape(1, nrec), weights,
    )
    return solutions.reshape(warm_start.shape), gradient


def solution(mesh):
    nsrc, ngx, nyz = (mesh.shape[name] for name in ("src", "gx", "yz"))

    def run(warm_start, conductivity, *rest):
        gx, gy, gz = conductivity.shape
        sizes = (nsrc, ngx, nyz, gx // ngx, gy // nyz, gz)
        return jax.shard_map(
            functools.partial(on_device, sizes),
            mesh=mesh,
            in_specs=(
                P(None, "src", "gx", "yz", None),
                P("gx", "yz", None),
                P("src"),
                P("src", None),
                P(),
                P("src", None),
            ),
            out_specs=(P(None, "src", "gx", "yz", None), P("gx", "yz", "src")),
            check_vma=False,
        )(warm_start, conductivity, *rest)

    return run
```

```python
import functools
import jax
import jax.numpy as jnp
from jax import lax
from jax.experimental import pallas as pl
from jax.experimental.pallas import tpu as pltpu
from jax.sharding import PartitionSpec as P

MESH = pl.DeviceIdType.MESH
F32 = jnp.float32
COLS = 8
PAIRS = [(a, b) for a in range(COLS) for b in range(a, COLS)]


def matmul8(left, right):
    total = left[:, 0:1] * right[0:1, :]
    for k in range(1, COLS):
        total = total + left[:, k : k + 1] * right[k : k + 1, :]
    return total


def inverse8(matrix, row, lane):
    work = jnp.where(lane < COLS, matrix, jnp.where(lane - COLS == row, 1.0, 0.0))
    for k in range(COLS):
        scaled = work[k : k + 1, :] / work[k : k + 1, k : k + 1]
        work = jnp.where(row == k, scaled, work - work[:, k : k + 1] * scaled)
    return pltpu.roll(work, 128 - COLS, 1)


def kernel(
    sizes,
    warm, cond, currents_in, electrodes_in, receivers_in, weights_in,
    out_x, out_g,
    currents, electrodes, receivers, weights,
    xv, pv, wv, yh, ysend, cv, ch, csend, cf, dv, iv, ybuf, onehot, table, gbuf, gp, grecv,
    load_sem, out_sem, send_sem, recv_sem, ysend_sem, yrecv_sem, csend_sem, crecv_sem, gram_send, gram_recv, grad_send, grad_recv,
):
    nsrc, ngx, nyz, nx, ny, nz = sizes
    count = COLS // 2
    src, gx, yz = lax.axis_index("src"), lax.axis_index("gx"), lax.axis_index("yz")
    group = ngx * nyz
    me = gx * nyz + yz

    load_c = pltpu.make_async_copy(cond, cv.at[pl.ds(1, nx)], load_sem.at[0])
    load_x = pltpu.make_async_copy(warm, xv.at[:, pl.ds(1, nx)], load_sem.at[1])
    small = [
        pltpu.make_async_copy(source, target, load_sem.at[2 + i])
        for i, (source, target) in enumerate((
            (currents_in, currents), (electrodes_in, electrodes), (receivers_in, receivers), (weights_in, weights),
        ))
    ]
    load_c.start()
    for copy in small:
        copy.start()
    load_x.start()

    barrier = pltpu.get_barrier_semaphore()
    for o in range(1, group):
        to = lax.rem(me + o, group)
        pl.semaphore_signal(
            barrier, inc=1, device_id={"gx": to // nyz, "yz": lax.rem(to, nyz)}, device_id_type=MESH
        )
    for o in range(1, nsrc):
        pl.semaphore_signal(
            barrier, inc=1, device_id={"src": lax.rem(src + o, nsrc)}, device_id_type=MESH
        )

    edges = (gx > 0, gx < ngx - 1, yz > 0, yz < nyz - 1)
    fields = (xv, pv, wv)
    parts = 4
    width = nx // parts

    for side, plane in ((0, 0), (1, nx + 1)):
        @pl.when(jnp.logical_not(edges[side]))
        def _(plane=plane):
            cv[plane] = jnp.zeros((ny, nz), F32)
            for ref in fields:
                for c in range(COLS):
                    ref[c, plane] = jnp.zeros((ny, nz), F32)

    for side in (0, 1):
        @pl.when(jnp.logical_not(edges[2 + side]))
        def _(side=side):
            ch[side] = jnp.zeros((nx, nz), F32)
            for phase in range(3):
                for c in range(COLS):
                    yh[phase, side, c] = jnp.zeros((nx, nz), F32)

    def remote(source, target, send, recv, where):
        return pltpu.make_async_remote_copy(
            src_ref=source, dst_ref=target, send_sem=send, recv_sem=recv,
            device_id=where, device_id_type=MESH,
        )

    def x_copies(source, phase):
        def cut(plane):
            return source.at[plane] if phase == 3 else source.at[:, plane]

        def mine(plane):
            return warm.at[:, plane - 1] if phase == 0 else cut(plane)
        if phase == 3:
            send, recv = csend_sem, crecv_sem
        else:
            send, recv = send_sem.at[phase], recv_sem.at[phase]
        return (
            (remote(mine(nx), cut(0), send.at[0], recv.at[0], {"gx": jnp.minimum(gx + 1, ngx - 1)}), edges[1], edges[0]),
            (remote(mine(1), cut(nx + 1), send.at[1], recv.at[1], {"gx": jnp.maximum(gx - 1, 0)}), edges[0], edges[1]),
        )

    after_y, before_y = {"yz": jnp.minimum(yz + 1, nyz - 1)}, {"yz": jnp.maximum(yz - 1, 0)}

    def c_copies():
        return (
            (remote(csend.at[1], ch.at[0], csend_sem.at[2], crecv_sem.at[2], after_y), edges[3], edges[2]),
            (remote(csend.at[0], ch.at[1], csend_sem.at[3], crecv_sem.at[3], before_y), edges[2], edges[3]),
        )

    def y_copies(phase, q):
        part = pl.ds(pl.multiple_of(q * width, 8), width)
        out, into = ysend.at[phase], yh.at[phase]
        send, recv = ysend_sem.at[phase, q], yrecv_sem.at[phase, q]
        return (
            (remote(out.at[1, :, part], into.at[0, :, part], send.at[0], recv.at[0], after_y), edges[3], edges[2]),
            (remote(out.at[0, :, part], into.at[1, :, part], send.at[1], recv.at[1], before_y), edges[2], edges[3]),
        )

    def sweep(phase, plane, carry):
        def part(k, carry):
            q = lax.rem(parts - k, parts)
            arrive(y_copies(phase, q))
            source = fields[phase]

            @pl.when(k == 0)
            def _():
                arrive(x_copies(source, phase)[:1])

            @pl.when(k == 1)
            def _():
                arrive(x_copies(source, phase)[1:])

            carry = lax.fori_loop(0, width, lambda i, c: plane(q * width + i, c), carry)
            if phase < 2:
                start(y_copies(phase + 1, q))
                target = fields[phase + 1]

                @pl.when(k == 0)
                def _():
                    start(x_copies(target, phase + 1)[1:])

                @pl.when(k == 1)
                def _():
                    start(x_copies(target, phase + 1)[:1])
            return carry

        return lax.fori_loop(0, parts, part, carry)

    def start(copies):
        for copy, sends, _ in copies:
            pl.when(sends)(copy.start)

    def arrive(copies):
        for copy, _, receives in copies:
            pl.when(receives)(copy.wait_recv)

    def finish(copies):
        for copy, sends, _ in copies:
            pl.when(sends)(copy.wait_send)

    pl.semaphore_wait(barrier, group - 1 + nsrc - 1)

    x_x = x_copies(xv, 0)
    start(x_x)
    load_c.wait()
    c_x = x_copies(cv, 3)
    start(c_x)
    for x in range(nx):
        csend[0, x : x + 1] = cv[x + 1, 0:1]
        csend[1, x : x + 1] = cv[x + 1, ny - 1 : ny]
    c_y = c_copies()
    start(c_y)

    load_x.wait()

    @pl.loop(0, nx)
    def _(x):
        for c in range(COLS):
            ysend[0, 0, c, pl.ds(x, 1)] = xv[c, x + 1, 0:1]
            ysend[0, 1, c, pl.ds(x, 1)] = xv[c, x + 1, ny - 1 : ny]

    for q in (0, 3, 2, 1):
        start(y_copies(0, q))
    for copy in small:
        copy.wait()

    row = lax.broadcasted_iota(jnp.int32, (ny, nz), 0)
    lane = lax.broadcasted_iota(jnp.int32, (ny, nz), 1)

    span = nyz * ny * nz
    place = receivers[...]
    where_x = place // span - gx * nx
    where_y = lax.rem(place, span) // nz - yz * ny
    inside = (where_x >= 0) & (where_x < nx) & (where_y >= 0) & (where_y < ny)
    line = jnp.where(inside, where_x * ny + where_y, -1)
    nrec = place.shape[1]
    spot = jnp.broadcast_to(lax.rem(place, nz), (nz, nrec))
    onehot[...] = jnp.where(
        lax.broadcasted_iota(jnp.int32, (nz, nrec), 0) == spot, 1.0, 0.0
    ).astype(jnp.bfloat16)
    step = 4
    rows = lax.broadcasted_iota(jnp.int32, (step * ny, nrec), 0)

    @pl.loop(0, nx // step)
    def _(i):
        match = rows + i * (step * ny) == line
        values = [weights[s : s + 1] for s in range(count)]
        total = None
        for part in range(2):
            pieces = [value.astype(jnp.bfloat16).astype(F32) for value in values]
            values = [value - piece for value, piece in zip(values, pieces)]
            term = lax.dot_general(
                jnp.concatenate([jnp.where(match, piece, 0.0).astype(jnp.bfloat16) for piece in pieces], axis=0),
                onehot[...], (((1,), (1,)), ((), ())), preferred_element_type=F32,
            )
            total = term if total is None else total + term
        for s in range(count):
            for j in range(step):
                first = (s * step + j) * ny
                pv[count + s, i * step + j + 1] = total[first : first + ny]

    arrive(c_x)
    arrive(c_y)

    @pl.loop(0, nx)
    def _(x):
        mid = cv[x + 1]
        near = (
            cv[x + 2],
            cv[x],
            jnp.where(row == ny - 1, ch[1, pl.ds(x, 1)], pltpu.roll(mid, ny - 1, 0)),
            jnp.where(row == 0, ch[0, pl.ds(x, 1)], pltpu.roll(mid, 1, 0)),
            jnp.where(lane == nz - 1, 0.0, pltpu.roll(mid, nz - 1, 1)),
            jnp.where(lane == 0, 0.0, pltpu.roll(mid, 1, 1)),
        )
        faces = [0.5 * (mid + value) for value in near]
        diagonal = faces[0]
        for value in faces[1:]:
            diagonal = diagonal + value
        inverse = 1.0 / diagonal
        dv[x] = diagonal
        iv[x] = inverse
        faces[4] = jnp.where(lane == nz - 1, 0.0, faces[4])
        faces[5] = jnp.where(lane == 0, 0.0, faces[5])
        for j in range(6):
            cf[j, x] = faces[j] * inverse

    def around(phase, c, x):
        ref = fields[phase]
        field = ref[c, x + 1]
        above = jnp.where(row == ny - 1, yh[phase, 1, c, pl.ds(x, 1)], pltpu.roll(field, ny - 1, 0))
        below = jnp.where(row == 0, yh[phase, 0, c, pl.ds(x, 1)], pltpu.roll(field, 1, 0))
        total = cf[0, x] * ref[c, x + 2] + cf[1, x] * ref[c, x]
        total = total + cf[2, x] * above
        total = total + cf[3, x] * below
        total = total + cf[4, x] * pltpu.roll(field, nz - 1, 1)
        total = total + cf[5, x] * pltpu.roll(field, 1, 1)
        return field, total

    def plane_p(x, carry):
        cell = row * nz + lane + ((gx * nx + x) * span + yz * (ny * nz))
        inverse = iv[x]
        for c in range(COLS):
            field, total = around(0, c, x)
            if c < count:
                amount = currents[c]
                source = jnp.where(cell == electrodes[0, c], amount, 0.0) - jnp.where(
                    cell == electrodes[1, c], amount, 0.0
                )
            else:
                source = pv[c, x + 1]
            value = source * inverse - field + total
            pv[c, x + 1] = value
            ysend[1, 0, c, pl.ds(x, 1)] = value[0:1]
            ysend[1, 1, c, pl.ds(x, 1)] = value[ny - 1 : ny]

        return carry

    sweep(0, plane_p, 0)

    def products(acc, x, left, right):
        acc = list(acc)
        for yb in range(ny // 8):
            for zb in range(nz // 128):
                cut = (slice(yb * 8, yb * 8 + 8), slice(zb * 128, zb * 128 + 128))
                scale = dv[(x,) + cut]
                lefts = [left[(a, x + 1) + cut] * scale for a in range(COLS)]
                if right is ybuf:
                    rights = [right[(b,) + cut] for b in range(COLS)]
                else:
                    rights = [right[(b, x + 1) + cut] for b in range(COLS)]
                for i, (a, b) in enumerate(PAIRS):
                    acc[i] = acc[i] + lefts[a] * rights[b]
        return tuple(acc)

    zeros = tuple(jnp.zeros((8, 128), F32) for _ in PAIRS)
    row8 = lax.broadcasted_iota(jnp.int32, (8, 128), 0)
    lane8 = lax.broadcasted_iota(jnp.int32, (8, 128), 1)

    def collect(acc):
        sums = {}
        for (a, b), value in zip(PAIRS, acc):
            sums[a, b] = sums[b, a] = jnp.sum(value, axis=0, keepdims=True)
        matrix = jnp.zeros((8, 128), F32)
        for a in range(COLS):
            block = jnp.zeros((8, 128), F32)
            for b in range(COLS):
                block = jnp.where(row8 == b, sums[a, b], block)
            matrix = jnp.where(lane8 == a, jnp.sum(block, axis=1, keepdims=True), matrix)
        return matrix

    def gram(left, right):
        return collect(lax.fori_loop(0, nx, lambda x, acc: products(acc, x, left, right), zeros))

    mine = gram(pv, pv)

    def plane_w(x, carry):
        for c in range(COLS):
            field, total = around(1, c, x)
            value = field - total
            wv[c, x + 1] = value
            ysend[2, 0, c, pl.ds(x, 1)] = value[0:1]
            ysend[2, 1, c, pl.ds(x, 1)] = value[ny - 1 : ny]

        return carry

    sweep(1, plane_w, 0)

    mine = mine + pltpu.roll(gram(pv, wv), 8, 1)
    mine = mine + pltpu.roll(gram(wv, wv), 16, 1)

    def last(x, acc):
        for c in range(COLS):
            field, total = around(2, c, x)
            ybuf[c] = field - total
        return products(acc, x, wv, ybuf)

    mine = mine + pltpu.roll(collect(sweep(2, last, zeros)), 24, 1)

    gbuf[me] = mine
    sums = []
    for o in range(1, group):
        to = lax.rem(me + o, group)
        copy = remote(
            gbuf.at[me], gbuf.at[me], gram_send.at[o - 1], gram_recv.at[o - 1],
            {"gx": to // nyz, "yz": lax.rem(to, nyz)},
        )
        copy.start()
        sums.append(copy)
    for copy in sums:
        copy.wait_recv()
    total = gbuf[0]
    for o in range(1, group):
        total = total + gbuf[o]

    first = total
    curve = pltpu.roll(total, 120, 1)
    second = pltpu.roll(total, 112, 1)
    third = pltpu.roll(total, 104, 1)
    unit = jnp.where(row8 == lane8, 1.0, 0.0)
    curve_inv = inverse8(curve, row8, lane8)
    first_inv = inverse8(first, row8, lane8)
    alpha = matmul8(curve_inv, first)
    alpha_t = matmul8(first, curve_inv)
    second_alpha = matmul8(second, alpha)
    fresh = first - matmul8(curve, alpha) - matmul8(alpha_t, curve) + matmul8(alpha_t, second_alpha)
    mixed = unit + matmul8(first_inv, fresh)
    mixed_t = unit + matmul8(fresh, first_inv)
    upper = matmul8(curve, mixed) - second_alpha
    lower = matmul8(second, mixed) - matmul8(third, alpha)
    curve_next = matmul8(mixed_t, upper) - matmul8(alpha_t, lower)
    alpha_next = matmul8(inverse8(curve_next, row8, lane8), fresh)
    coef_p = alpha + matmul8(mixed, alpha_next)
    coef_w = -matmul8(alpha, alpha_next)
    for a in range(COLS):
        for b in range(COLS):
            table[a * COLS + b] = jnp.broadcast_to(coef_p[a : a + 1, b : b + 1], (8, 128))
            table[(COLS + a) * COLS + b] = jnp.broadcast_to(coef_w[a : a + 1, b : b + 1], (8, 128))

    def combine(xref, pref, wref, index, cuts):
        starts = [[ref[(a,) + index + cut] for a in range(COLS) for cut in cuts] for ref in (pref, wref)]
        n = len(cuts)
        for b in range(COLS):
            acc = [xref[(b,) + index + cut] for cut in cuts]
            for part in range(2):
                for a in range(COLS):
                    factor = table[(part * COLS + a) * COLS + b]
                    acc = [acc[j] + starts[part][a * n + j] * factor for j in range(n)]
            for j, cut in enumerate(cuts):
                xref[(b,) + index + cut] = acc[j]

    finish(x_x)
    lanes = [slice(zb * 128, zb * 128 + 128) for zb in range(nz // 128)]

    @pl.loop(0, nx + 2)
    def _(x):
        for yb in range(ny // 8):
            combine(xv, pv, wv, (x,), [(slice(yb * 8, yb * 8 + 8), cut) for cut in lanes])

    for side in (0, 1):
        @pl.when(edges[2 + side])
        def _(side=side):
            @pl.loop(0, nx // 8)
            def _(i):
                combine(
                    yh.at[0, side], yh.at[1, side], yh.at[2, side], (),
                    [(pl.ds(pl.multiple_of(i * 8, 8), 8), cut) for cut in lanes],
                )

    store_x = pltpu.make_async_copy(xv.at[:, pl.ds(1, nx)], out_x, out_sem)

    store_x.start()

    half = lane8 < 64
    chunks = 8
    length = nx // chunks

    def face(x):
        total = None
        for s in range(count):
            term = (xv[s, x] - xv[s, x + 1]) * (xv[count + s, x] - xv[count + s, x + 1])
            total = term if total is None else total + term
        return total

    def planes(x, before):
        after = face(x + 1)
        fy = fz = edge_y = edge_z = None
        for s in range(count):
            u, w = xv[s, x + 1], xv[count + s, x + 1]
            uy = u - jnp.where(row == ny - 1, yh[0, 1, s, pl.ds(x, 1)], pltpu.roll(u, ny - 1, 0))
            wy = w - jnp.where(row == ny - 1, yh[0, 1, count + s, pl.ds(x, 1)], pltpu.roll(w, ny - 1, 0))
            uz = u - jnp.where(lane == nz - 1, 0.0, pltpu.roll(u, nz - 1, 1))
            wz = w - jnp.where(lane == nz - 1, 0.0, pltpu.roll(w, nz - 1, 1))
            low = (u[0:1] - yh[0, 0, s, pl.ds(x, 1)]) * (w[0:1] - yh[0, 0, count + s, pl.ds(x, 1)])
            terms = (uy * wy, uz * wz, low, u * w)
            if fy is None:
                fy, fz, edge_y, edge_z = terms
            else:
                fy, fz, edge_y, edge_z = (p + q for p, q in zip((fy, fz, edge_y, edge_z), terms))
        total = before + after
        total = total + fy + jnp.where(row == 0, edge_y, pltpu.roll(fy, 1, 0))
        total = total + fz + jnp.where(lane == 0, edge_z, pltpu.roll(fz, 1, 1))
        total = -0.5 * total
        for t in range(nz // 128):
            top, low = total[0:8, lanes[t]], total[8:16, lanes[t]]
            gp[2 * t, x] = jnp.where(half, top, pltpu.roll(low, 64, 1))
            gp[2 * t + 1, x] = jnp.where(half, pltpu.roll(top, 64, 1), low)
        return after

    def grad_copies(k):
        part = pl.ds(k * length, length)
        for o in range(1, nsrc):
            to = lax.rem(src + o, nsrc)
            yield remote(
                gp.at[to, part], grecv.at[o - 1, part],
                grad_send.at[k, o - 1], grad_recv.at[k, o - 1], {"src": to},
            )

    def send_chunk(k, before):
        before = lax.fori_loop(k * length, (k + 1) * length, planes, before)
        for copy in grad_copies(k):
            copy.start()
        return before

    lax.fori_loop(0, chunks, send_chunk, face(0))

    @pl.loop(0, chunks)
    def _(k):
        for copy in grad_copies(k):
            copy.wait_recv()
        for i in range(length):
            x = k * length + i
            total = gp[src, x]
            for o in range(nsrc - 1):
                total = total + grecv[o, x]
            out_g[x, 0:8] = total[:, 0:64]
            out_g[x, 8:16] = pltpu.roll(total, 64, 1)[:, 0:64]

    @pl.loop(0, chunks)
    def _(k):
        for copy in grad_copies(k):
            copy.wait_send()

    for copies in (c_x, c_y, x_copies(pv, 1), x_copies(wv, 2)):
        finish(copies)
    for phase in range(3):
        for q in range(parts):
            finish(y_copies(phase, q))
    for copy in sums:
        copy.wait_send()
    store_x.wait()


def on_device(sizes, warm_start, conductivity, currents, electrodes, receivers, weights):
    nsrc, ngx, nyz, nx, ny, nz = sizes
    group = ngx * nyz
    nrec = receivers.shape[0]
    count = weights.shape[0]
    dma = pltpu.SemaphoreType.DMA
    vmem = pl.BlockSpec(memory_space=pltpu.VMEM)
    hbm = pl.BlockSpec(memory_space=pltpu.HBM)
    block = pltpu.VMEM((COLS, nx + 2, ny, nz), F32)
    cells = COLS * nx * ny * nz
    solutions, gradient = pl.pallas_call(
        functools.partial(kernel, sizes),
        out_shape=(
            pltpu.VMEM((COLS, nx, ny, nz), F32),
            pltpu.VMEM((nx, ny, nz // nsrc), F32),
        ),
        in_specs=[hbm] * 6,
        out_specs=(hbm, vmem),
        scratch_shapes=[
            pltpu.SMEM((count,), F32),
            pltpu.SMEM((2, count), jnp.int32),
            pltpu.VMEM((1, nrec), jnp.int32),
            pltpu.VMEM((count, nrec), F32),
            block, block, block,
            pltpu.VMEM((3, 2, COLS, nx, nz), F32),
            pltpu.VMEM((3, 2, COLS, nx, nz), F32),
            pltpu.VMEM((nx + 2, ny, nz), F32),
            pltpu.VMEM((2, nx, nz), F32),
            pltpu.VMEM((2, nx, nz), F32),
            pltpu.VMEM((6, nx, ny, nz), F32),
            pltpu.VMEM((nx, ny, nz), F32),
            pltpu.VMEM((nx, ny, nz), F32),
            pltpu.VMEM((COLS, ny, nz), F32),
            pltpu.VMEM((nz, nrec), jnp.bfloat16),
            pltpu.VMEM((2 * COLS * COLS, 8, 128), F32),
            pltpu.VMEM((group, 8, 128), F32),
            pltpu.VMEM((nsrc, nx, 8, 128), F32),
            pltpu.VMEM((nsrc - 1, nx, 8, 128), F32),
            dma((6,)), dma,
            dma((3, 2)), dma((3, 2)),
            dma((3, 4, 2)), dma((3, 4, 2)),
            dma((4,)), dma((4,)),
            dma((group - 1,)), dma((group - 1,)),
            dma((8, nsrc - 1)), dma((8, nsrc - 1)),
        ],
        compiler_params=pltpu.CompilerParams(
            collective_id=0, has_side_effects=True, vmem_limit_bytes=56 * 1024 * 1024
        ),
        cost_estimate=pl.CostEstimate(flops=300 * cells, bytes_accessed=8 * cells, transcendentals=0),
    )(
        warm_start.reshape((COLS, nx, ny, nz)), conductivity, currents, electrodes.T,
        receivers.reshape(1, nrec), weights,
    )
    return solutions.reshape(warm_start.shape), gradient


def solution(mesh):
    nsrc, ngx, nyz = (mesh.shape[name] for name in ("src", "gx", "yz"))

    def run(warm_start, conductivity, *rest):
        gx, gy, gz = conductivity.shape
        sizes = (nsrc, ngx, nyz, gx // ngx, gy // nyz, gz)
        return jax.shard_map(
            functools.partial(on_device, sizes),
            mesh=mesh,
            in_specs=(
                P(None, "src", "gx", "yz", None),
                P("gx", "yz", None),
                P("src"),
                P("src", None),
                P(),
                P("src", None),
            ),
            out_specs=(P(None, "src", "gx", "yz", None), P("gx", "yz", "src")),
            check_vma=False,
        )(warm_start, conductivity, *rest)

    return run
```
